32 devices in a mesh: row: 16 (over z, x, core), col: 2 (over y).
Axes of the slice: x: 2, y: 2, z: 4, core: 2. Of those that a mesh axis runs over, the one named last changes fastest.
Arguments:
- alignment_activations: bfloat16 [64, 768, 256], P(None, ('row', 'col')), may hold values from -60 to 60
- layer_norm_gain: float32 [256], replicated, may hold values from 0.5 to 1.5
- layer_norm_bias: float32 [256], replicated, may hold values from -3 to 3
- left_weight: bfloat16 [256, 32], replicated, may hold values from -0.375 to 0.375
- left_operand_bias: float32 [32], replicated, may hold values from -3 to 3
- right_weight: bfloat16 [256, 32], replicated, may hold values from -0.375 to 0.375
- right_operand_bias: float32 [32], replicated, may hold values from -3 to 3
- output_weight: bfloat16 [1024, 128], replicated, may hold values from -0.75 to 0.75
- output_bias_vector: float32 [128], replicated, may hold values from -3 to 3
- pair_cotangent: bfloat16 [768, 768, 128], P('row', 'col'), may hold values from -6 to 6
Outputs:
- pair_output_update: bfloat16 [768, 768, 128], P('row', 'col')
- alignment_gradient: bfloat16 [64, 768, 256], P(None, ('row', 'col'))
- output_weight_gradient: float32 [1024, 128], replicated
The draws below stay inside these ranges and needn't reach their ends.
All inputs are finite; a program needn't handle non-finite values.
Results may differ from the reference program's by a relative error of at most 0.028.
Values may be sent and summed in bfloat16 or wider, within the bound.
A program may use at most 64 MiB of HBM per device.

```python
import math
import jax
import jax.numpy as jnp
from jax import lax

CM = 256
CH = 32
PAIR = 128
S = 64
IBLK = 8
R = 768


def draw_alignment_activations(key, part):
    key = jax.random.fold_in(key, 11)
    first_key, second_key, third_key = jax.random.split(key, 3)
    base = jnp.clip(jax.random.normal(first_key, (S, R, CM), jnp.float32), -4.0, 4.0)
    spread = jnp.exp(jax.random.uniform(second_key, (S, R, 1), jnp.float32, 0.0, math.log(10.0)))
    offset = jnp.clip(0.3 * jax.random.normal(third_key, (1, R, CM), jnp.float32), -1.0, 1.0)
    return ((base + offset) * spread).astype(jnp.bfloat16)


def raised(values, rng, source, target, blocks, factor):
    def block_of(position):
        return (jnp.arange(values.shape[position]) // (values.shape[position] // blocks)).reshape((-1,) + (1,) * (values.ndim - 1 - position))

    near = jax.random.permutation(rng, blocks)[block_of(target)]
    other_side = (block_of(target) + blocks // 2) % blocks
    return jnp.where((block_of(source) == near) | (block_of(source) == other_side), factor * values, values)


def block_scale(own_key, extent, cuts, low, top_value):
    factor_of = 1.0
    for position, parts in cuts:
        heights = jax.random.uniform(jax.random.fold_in(jax.random.fold_in(own_key, 6), position), (parts,), jnp.float32, low / len(cuts), top_value / len(cuts))
        factor_of = factor_of * jnp.repeat(jnp.exp(heights), extent[position] // parts).reshape((-1,) + (1,) * (len(extent) - 1 - position))
    return factor_of


def noise(own_key, dims, width, bound, cuts=(), dtype=jnp.bfloat16):
    array = width * jax.random.normal(own_key, dims, jnp.float32)
    if cuts:
        array = array * block_scale(own_key, dims, cuts, -0.22, 0.18)
    return jnp.clip(array, -bound, bound).astype(dtype)


def heavy_noise(stream_key, dims, scale, bound, cuts, heavy, dtype=jnp.bfloat16):
    values = scale * jax.random.normal(stream_key, dims, jnp.float32)
    if cuts:
        values = values * block_scale(stream_key, dims, cuts, -0.22, 0.18)
    return jnp.clip(raised(values, jax.random.fold_in(stream_key, 3), *heavy), -bound, bound).astype(dtype)


def setup_inputs(seed: int = 0) -> dict:
    arg_keys = jax.random.split(jax.random.key(seed), 11)
    alignment_activations = draw_alignment_activations(jax.random.fold_in(arg_keys[10], 71), 0)
    layer_norm_gain = jnp.clip(jax.random.uniform(arg_keys[1], (CM,), jnp.float32, 0.5, 1.5), 0.5, 1.5)
    layer_norm_bias = noise(arg_keys[2], (CM,), 0.5, 3.0, (), jnp.float32)
    left_weight = noise(arg_keys[3], (CM, CH), CM ** -0.5, 0.375)
    left_operand_bias = noise(arg_keys[4], (CH,), 0.5, 3.0, (), jnp.float32)
    right_weight = noise(arg_keys[5], (CM, CH), CM ** -0.5, 0.375)
    right_operand_bias = noise(arg_keys[6], (CH,), 0.5, 3.0, (), jnp.float32)
    output_weight = noise(arg_keys[7], (CH * CH, PAIR), 64 ** -0.5, 0.75)
    output_bias_vector = noise(arg_keys[8], (PAIR,), 0.5, 3.0, (), jnp.float32)
    pair_cotangent = heavy_noise(arg_keys[9], (R, R, PAIR), 1.0, 6.0, ((0, 16), (1, 2)), (0, 1, 16, 2.0))
    return dict(alignment_activations=alignment_activations, layer_norm_gain=layer_norm_gain, layer_norm_bias=layer_norm_bias, left_weight=left_weight, left_operand_bias=left_operand_bias, right_weight=right_weight, right_operand_bias=right_operand_bias, output_weight=output_weight, output_bias_vector=output_bias_vector, pair_cotangent=pair_cotangent)


def apply_layer_norm(alignment_activations, layer_norm_gain, layer_norm_bias):
    input_values = alignment_activations.astype(jnp.float32)
    average = lax.optimization_barrier(jnp.mean(input_values, axis=-1, keepdims=True))
    shifted = input_values - average
    variance = lax.optimization_barrier(jnp.mean(shifted * shifted, axis=-1, keepdims=True))
    inverse_deviation = lax.rsqrt(variance + 1e-05)
    standardized_input = shifted * inverse_deviation
    normalized_input = (standardized_input * layer_norm_gain + layer_norm_bias).astype(jnp.bfloat16)
    return (standardized_input, inverse_deviation, normalized_input)

def project(normalized_input, weight, bias_vec):
    sequence_count, residue_count, alignment_width = normalized_input.shape
    flattened_row_matrix = normalized_input.reshape(-1, alignment_width)
    result = jnp.dot(flattened_row_matrix, weight, preferred_element_type=jnp.float32) + bias_vec
    return result.astype(jnp.bfloat16).reshape(sequence_count, residue_count, weight.shape[1])

def reference(alignment_activations, layer_norm_gain, layer_norm_bias, left_weight, left_operand_bias, right_weight, right_operand_bias, output_weight, output_bias_vector, pair_cotangent):
    standardized_input, inverse_deviation, normalized_input = apply_layer_norm(alignment_activations, layer_norm_gain, layer_norm_bias)
    left_proj = project(normalized_input, left_weight, left_operand_bias)
    right_proj = project(normalized_input, right_weight, right_operand_bias)
    right_wide = right_proj.astype(jnp.float32)
    factor = 1.0 / S
    blocks = R // IBLK
    row_blocks = left_proj.reshape(S, blocks, IBLK, CH).transpose(1, 0, 2, 3)
    grad_blocks = pair_cotangent.reshape(blocks, IBLK, R, PAIR)

    def block_step(carry, pieces):
        right_acc, weight_acc = carry
        row_block, grad_block = pieces
        row_wide = row_block.astype(jnp.float32)
        outer_sum = jnp.einsum('sip,sjq->ijpq', row_wide, right_wide)
        outer_mean = (outer_sum * factor).astype(jnp.bfloat16)
        flat_outer = outer_mean.reshape(-1, CH * CH)
        update = jnp.dot(flat_outer, output_weight, preferred_element_type=jnp.float32) + output_bias_vector
        update = update.astype(jnp.bfloat16).reshape(IBLK, R, PAIR)
        flat_grad = grad_block.reshape(-1, PAIR)
        weight_acc = weight_acc + jnp.dot(flat_outer.T, flat_grad, preferred_element_type=jnp.float32)
        outer_grad = jnp.dot(flat_grad, output_weight.T, preferred_element_type=jnp.float32)
        outer_grad = outer_grad.astype(jnp.bfloat16).reshape(IBLK, R, CH, CH)
        grad_wide = outer_grad.astype(jnp.float32)
        left_block = jnp.einsum('ijpq,sjq->sip', grad_wide, right_wide) * factor
        right_acc = right_acc + jnp.einsum('ijpq,sip->sjq', grad_wide, row_wide) * factor
        return ((right_acc, weight_acc), (update, left_block))
    initial = (jnp.zeros((S, R, CH), jnp.float32), jnp.zeros((CH * CH, PAIR), jnp.float32))
    (right_grad, output_weight_gradient), (updates, left_blocks) = lax.scan(block_step, initial, (row_blocks, grad_blocks))
    pair_output_update = updates.reshape(R, R, PAIR)
    left_grad = left_blocks.transpose(1, 0, 2, 3).reshape(S, R, CH)
    normalized_gradient = jnp.dot(left_grad.astype(jnp.bfloat16).reshape(-1, CH), left_weight.T, preferred_element_type=jnp.float32)
    normalized_gradient = normalized_gradient + jnp.dot(right_grad.astype(jnp.bfloat16).reshape(-1, CH), right_weight.T, preferred_element_type=jnp.float32)
    normalized_gradient = normalized_gradient.reshape(S, R, CM)
    scaled_gradient = normalized_gradient * layer_norm_gain
    centering_term = lax.optimization_barrier(jnp.mean(scaled_gradient, axis=-1, keepdims=True))
    gradient_slope_term = lax.optimization_barrier(jnp.mean(scaled_gradient * standardized_input, axis=-1, keepdims=True))
    alignment_gradient = (inverse_deviation * (scaled_gradient - centering_term - standardized_input * gradient_slope_term)).astype(jnp.bfloat16)
    return (pair_output_update, alignment_gradient, output_weight_gradient)
```

```python
import functools

import jax
import jax.numpy as jnp
from jax import lax
from jax.experimental import pallas as pl
from jax.experimental.pallas import tpu as pltpu
from jax.sharding import PartitionSpec as P

BF = jnp.bfloat16
F32 = jnp.float32


def divisor_up_to(total, most):
    best = 1
    for d in range(1, most + 1):
        if total % d == 0:
            best = d
    return best


def nn(a, b):
    return lax.dot_general(a, b, (((1,), (0,)), ((), ())), preferred_element_type=F32)


def nt(a, b):
    return lax.dot_general(a, b, (((1,), (1,)), ((), ())), preferred_element_type=F32)


def mix_kernel(ib, seqs, hidden, l_ref, w_ref, dp_ref, m_ref, dr_ref, acc, wide):
    step = pl.program_id(0)
    out = dp_ref.shape[2]
    rows = l_ref[...]
    for q in range(0, hidden, 2):
        res = nn(rows, w_ref[:, q * out : (q + 2) * out]).astype(BF)
        for e in range(2):
            for i in range(ib):
                m_ref[(q + e) * seqs : (q + e + 1) * seqs, i * out : (i + 1) * out] = res[
                    i * seqs : (i + 1) * seqs, e * out : (e + 1) * out
                ]
    for i in range(ib):
        wide[:, i * out : (i + 1) * out] = dp_ref[i]

    @pl.when(step == 0)
    def _():
        acc[...] = jnp.zeros_like(acc)

    width = 256
    for c in range(0, hidden * seqs, width):
        acc[:, c : c + width] += nt(wide[...], m_ref[c : c + width, :])

    @pl.when(step == pl.num_programs(0) - 1)
    def _():
        dr_ref[...] = acc[...].astype(BF)


def grad_kernel(ib, seqs, hidden, rt_ref, dp_ref, wt_ref, lt_ref, dl_ref, dw_ref, nl, wide):
    step = pl.program_id(0)
    out = dp_ref.shape[2]
    for i in range(ib):
        wide[:, i * out : (i + 1) * out] = dp_ref[i]
    qs = 4
    for q in range(0, hidden, qs):
        res = nn(rt_ref[q * seqs : (q + qs) * seqs, :], wide[...]).astype(BF)
        for e in range(qs):
            for i in range(ib):
                nl[i * seqs : (i + 1) * seqs, (q + e) * out : (q + e + 1) * out] = res[
                    e * seqs : (e + 1) * seqs, i * out : (i + 1) * out
                ]
    dl_ref[...] = nn(nl[...], wt_ref[...]).astype(BF)

    @pl.when(step == 0)
    def _():
        dw_ref[...] = jnp.zeros_like(dw_ref)

    width = 512
    for c in range(0, hidden * out, width):
        dw_ref[:, c : c + width] += nn(lt_ref[...], nl[:, c : c + width])


def update_kernel(ib, r_ref, m_ref, b_ref, o_ref):
    out = o_ref.shape[2]
    for i in range(0, ib, 2):
        res = nn(r_ref[...], m_ref[:, i * out : (i + 2) * out])
        for e in range(2):
            o_ref[i + e] = (res[:, e * out : (e + 1) * out] + b_ref[...]).astype(BF)


def apply_layer_norm(x, gain, bias):
    v = x.astype(F32)
    average = jnp.mean(v, axis=-1, keepdims=True)
    shifted = v - average
    variance = jnp.mean(shifted * shifted, axis=-1, keepdims=True)
    inv = lax.rsqrt(variance + 1e-05)
    standard = shifted * inv
    return standard, inv, (standard * gain + bias).astype(BF)


def local(x, gain, bias, wl, bl, wr, br, wo, bo, dp):
    seqs, own, width = x.shape
    hidden = wl.shape[1]
    out = wo.shape[1]
    nrow, ncol = lax.axis_size("row"), lax.axis_size("col")
    rows, cols, _ = dp.shape
    qs = hidden * seqs
    qh = hidden * out
    factor = 1.0 / seqs

    standard, inv, normed = apply_layer_norm(x, gain, bias)
    both = nn(normed.reshape(-1, width), jnp.concatenate([wl, wr], axis=1))
    left = (both[:, :hidden] + bl).astype(BF).reshape(seqs, own, hidden)
    right = (both[:, hidden:] + br).astype(BF).reshape(seqs, own, hidden)

    left_rows = lax.all_gather(left.transpose(1, 0, 2), "col", axis=0, tiled=True)
    left_rows = left_rows.reshape(rows * seqs, hidden)

    there = [(g, (g % nrow) * ncol + g // nrow) for g in range(nrow * ncol)]
    back = [(d, g) for g, d in there]
    mine = lax.ppermute(right.transpose(1, 2, 0).reshape(own, qs), ("row", "col"), there)
    right_cols = lax.all_gather(mine, "row", axis=0, tiled=True)
    right_t = (right_cols * BF(factor)).T

    w2 = wo.reshape(hidden, qh)
    ib = divisor_up_to(rows, 4)
    steps = rows // ib
    params = pltpu.CompilerParams(vmem_limit_bytes=56 * 1024 * 1024)

    m, dr = pl.pallas_call(
        functools.partial(mix_kernel, ib, seqs, hidden),
        grid=(steps,),
        in_specs=[
            pl.BlockSpec((ib * seqs, hidden), lambda t: (t, 0)),
            pl.BlockSpec((hidden, qh), lambda t: (0, 0)),
            pl.BlockSpec((ib, cols, out), lambda t: (t, 0, 0)),
        ],
        out_specs=[
            pl.BlockSpec((qs, ib * out), lambda t: (0, t)),
            pl.BlockSpec((cols, qs), lambda t: (0, 0)),
        ],
        out_shape=[
            jax.ShapeDtypeStruct((qs, rows * out), BF),
            jax.ShapeDtypeStruct((cols, qs), BF),
        ],
        scratch_shapes=[pltpu.VMEM((cols, qs), F32), pltpu.VMEM((cols, ib * out), BF)],
        compiler_params=params,
        cost_estimate=pl.CostEstimate(flops=2 * cols * qs * rows * out, bytes_accessed=30000000, transcendentals=0),
        name="mix",
    )(left_rows, w2 * BF(factor), dp)

    dr_mine = lax.psum_scatter(dr, "row", scatter_dimension=0, tiled=True)
    dr_own = lax.ppermute(dr_mine, ("row", "col"), back)

    dl, dw = pl.pallas_call(
        functools.partial(grad_kernel, ib, seqs, hidden),
        grid=(steps,),
        in_specs=[
            pl.BlockSpec((qs, cols), lambda t: (0, 0)),
            pl.BlockSpec((ib, cols, out), lambda t: (t, 0, 0)),
            pl.BlockSpec((qh, hidden), lambda t: (0, 0)),
            pl.BlockSpec((hidden, ib * seqs), lambda t: (0, t)),
        ],
        out_specs=[
            pl.BlockSpec((ib * seqs, hidden), lambda t: (t, 0)),
            pl.BlockSpec((hidden, qh), lambda t: (0, 0)),
        ],
        out_shape=[
            jax.ShapeDtypeStruct((rows * seqs, hidden), BF),
            jax.ShapeDtypeStruct((hidden, qh), F32),
        ],
        scratch_shapes=[pltpu.VMEM((ib * seqs, qh), BF), pltpu.VMEM((cols, ib * out), BF)],
        compiler_params=params,
        cost_estimate=pl.CostEstimate(flops=2 * cols * qs * rows * out, bytes_accessed=10000000, transcendentals=0),
        name="grad",
    )(right_t, dp, w2.T, left_rows.T)

    dl_own = lax.psum_scatter(
        dl.reshape(rows, seqs * hidden), "col", scatter_dimension=0, tiled=True
    )
    dw_all = lax.psum(dw, ("row", "col"))

    update = pl.pallas_call(
        functools.partial(update_kernel, ib),
        grid=(steps,),
        in_specs=[
            pl.BlockSpec((cols, qs), lambda t: (0, 0)),
            pl.BlockSpec((qs, ib * out), lambda t: (0, t)),
            pl.BlockSpec((1, out), lambda t: (0, 0)),
        ],
        out_specs=pl.BlockSpec((ib, cols, out), lambda t: (t, 0, 0)),
        out_shape=jax.ShapeDtypeStruct((rows, cols, out), BF),
        compiler_params=params,
        cost_estimate=pl.CostEstimate(flops=2 * cols * qs * rows * out, bytes_accessed=30000000, transcendentals=0),
        name="update",
    )(right_cols, m, bo.reshape(1, out))

    dl3 = dl_own.reshape(own, seqs, hidden).transpose(1, 0, 2).reshape(-1, hidden)
    dr3 = dr_own.reshape(own, hidden, seqs).transpose(2, 0, 1).reshape(-1, hidden)
    g = nt(jnp.concatenate([dl3, dr3], axis=1), jnp.concatenate([wl, wr], axis=1))
    g = g.reshape(seqs, own, width) * gain
    centre = jnp.mean(g, axis=-1, keepdims=True)
    slope = jnp.mean(g * standard, axis=-1, keepdims=True)
    dx = (inv * (g - centre - standard * slope)).astype(BF)
    return update, dx, dw_all.reshape(hidden * hidden, out)


def solution(mesh):
    both = ("row", "col")
    in_specs = (P(None, both, None),) + (P(),) * 8 + (P("row", "col", None),)
    out_specs = (P("row", "col", None), P(None, both, None), P())
    return jax.shard_map(local, mesh=mesh, in_specs=in_specs, out_specs=out_specs, check_vma=False)
```

```python
import functools

import jax
import jax.numpy as jnp
from jax import lax
from jax.experimental import pallas as pl
from jax.experimental.pallas import tpu as pltpu
from jax.sharding import PartitionSpec as P

BF = jnp.bfloat16
F32 = jnp.float32
MESH = pl.DeviceIdType.MESH


def divisor_up_to(total, most):
    best = 1
    for d in range(1, most + 1):
        if total % d == 0:
            best = d
    return best


def nn(a, b):
    return lax.dot_general(a, b, (((1,), (0,)), ((), ())), preferred_element_type=F32)


def nt(a, b):
    return lax.dot_general(a, b, (((1,), (1,)), ((), ())), preferred_element_type=F32)


def greet_all(me, ncol, total):
    barrier = pltpu.get_barrier_semaphore()

    def hello(k, carry):
        other = lax.rem(me + k, total)
        pl.semaphore_signal(barrier, inc=1, device_id=(other // ncol, lax.rem(other, ncol)), device_id_type=MESH)
        return carry

    lax.fori_loop(1, total, hello, 0)
    pl.semaphore_wait(barrier, total - 1)


def place(sizes):
    nrow, ncol = sizes
    r, c = lax.axis_index("row"), lax.axis_index("col")
    return r, c, r * ncol + c


def remote(src, dst, send, recv, row, col):
    return pltpu.make_async_remote_copy(
        src_ref=src, dst_ref=dst, send_sem=send, recv_sem=recv, device_id=(row, col), device_id_type=MESH
    )


def mix_kernel(sizes, ib, seqs, hidden, lt_ref, r_ref, w_ref, dp_ref, m_ref, dr_ref, ltall_ref, rall_ref,
               acc, wide, lbuf, lall, rbuf, lsend, lrecv, rsend, rrecv, fsend, own_sem):
    nrow, ncol = sizes
    half = nrow // 2
    r, c, me = place(sizes)
    step = pl.program_id(0)
    last = pl.num_programs(0) - 1
    out = dp_ref.shape[2]
    own, span = r_ref.shape[0], lt_ref.shape[1]
    par = lax.rem(r, 2)
    sib = r + 1 - 2 * par
    slot, block = lax.rem(me, nrow), me // nrow
    spar = lax.rem(slot, 2)

    def left_to(k):
        to = lax.rem(c + k, ncol)
        return remote(lt_ref, lbuf.at[c], lsend.at[k], lrecv.at[c], r, to)

    def left_from(k):
        fr = lax.rem(c + k, ncol)
        return remote(lt_ref, lbuf.at[fr], lsend.at[k], lrecv.at[fr], r, fr)

    def right_to(k):
        return remote(r_ref, rbuf.at[slot], rsend.at[k], rrecv.at[slot], 2 * k + spar, block)

    def is_me(k):
        return (block == c) & (2 * k + spar == r)

    def right_from(s):
        return remote(r_ref, rbuf.at[s], rsend.at[0], rrecv.at[s], sib, c)

    def forward(k):
        s = 2 * k + par
        return remote(rbuf.at[s], rbuf.at[s], fsend.at[k], rrecv.at[s], sib, c)

    keep = pltpu.make_async_copy(r_ref, rbuf.at[slot], own_sem)

    @pl.when(step == 0)
    def _():
        acc[...] = jnp.zeros_like(acc)
        greet_all(me, ncol, nrow * ncol)
        for k in range(1, ncol):
            left_to(k).start()
        for k in range(half):
            @pl.when(is_me(k))
            def _():
                keep.start()

            @pl.when(jnp.logical_not(is_me(k)))
            def _():
                right_to(k).start()
        lbuf[c] = lt_ref[...]
        for k in range(1, ncol):
            left_from(k).wait_recv()
        for k in range(ncol):
            ltall_ref[:, k * span : (k + 1) * span] = lbuf[k]
            lall[k * span : (k + 1) * span, :] = lbuf[k].astype(F32).T.astype(BF)

    rows = lall[pl.ds(pl.multiple_of(step * (ib * seqs), ib * seqs), ib * seqs), :]
    for q in range(0, hidden, 2):
        res = nn(rows, w_ref[:, q * out : (q + 2) * out]).astype(BF)
        for e in range(2):
            for i in range(ib):
                m_ref[(q + e) * seqs : (q + e + 1) * seqs, i * out : (i + 1) * out] = res[
                    i * seqs : (i + 1) * seqs, e * out : (e + 1) * out
                ]
    for i in range(ib):
        wide[:, i * out : (i + 1) * out] = dp_ref[i]
    width = 256
    for w in range(0, hidden * seqs, width):
        acc[:, w : w + width] += nt(wide[...], m_ref[w : w + width, :])

    @pl.when(step == last - 1)
    def _():
        for k in range(half):
            mine = c * nrow + 2 * k + par == me

            @pl.when(mine)
            def _():
                keep.wait()

            @pl.when(jnp.logical_not(mine))
            def _():
                right_from(2 * k + par).wait_recv()

            forward(k).start()

    @pl.when(step == last)
    def _():
        for k in range(nrow):
            dr_ref[k // 2, k % 2] = acc[k * own : (k + 1) * own, :].astype(BF)
        for k in range(half):
            right_from(2 * k + 1 - par).wait_recv()
            forward(k).wait_send()

            @pl.when(jnp.logical_not(is_me(k)))
            def _():
                right_to(k).wait_send()
        for k in range(1, ncol):
            left_to(k).wait_send()
        rall_ref[...] = rbuf[...]


def grad_kernel(sizes, ib, seqs, hidden, rt_ref, dp_ref, wt_ref, lt_ref, dr_ref, dl_ref, dw_ref, own_ref,
                nl, wide, mine, theirs, part, sum_sem, a_send, a_recv, b_send, b_recv, keep_sem):
    nrow, ncol = sizes
    half = nrow // 2
    r, c, me = place(sizes)
    step = pl.program_id(0)
    last = pl.num_programs(0) - 1
    out = dp_ref.shape[2]
    par = lax.rem(r, 2)
    sib = r + 1 - 2 * par
    slot, block = lax.rem(me, nrow), me // nrow
    spar = lax.rem(slot, 2)
    place_of = r // 2

    to_sib = remote(dr_ref.at[:, 1 - par], theirs, a_send, a_recv, sib, c)
    load = pltpu.make_async_copy(dr_ref.at[:, par], mine, sum_sem)

    def owner(k):
        g = c * nrow + 2 * k + par
        return g

    def to_owner(k):
        g = owner(k)
        return remote(mine.at[k], part.at[place_of], b_send.at[k], b_recv.at[place_of], g // ncol, lax.rem(g, ncol))

    def keep(k):
        return pltpu.make_async_copy(mine.at[k], part.at[place_of], keep_sem)

    def from_row(k):
        return remote(mine.at[0], part.at[k], b_send.at[0], b_recv.at[k], 2 * k + spar, block)

    @pl.when(step == 0)
    def _():
        greet_all(me, ncol, nrow * ncol)
        to_sib.start()
        load.start()
        dw_ref[...] = jnp.zeros_like(dw_ref)

    @pl.when(step == 1)
    def _():
        load.wait()
        to_sib.wait_recv()
        for k in range(half):
            mine[k] = (mine[k].astype(F32) + theirs[k].astype(F32)).astype(BF)
        for k in range(half):
            @pl.when(owner(k) == me)
            def _():
                keep(k).start()

            @pl.when(owner(k) != me)
            def _():
                to_owner(k).start()

    for i in range(ib):
        wide[:, i * out : (i + 1) * out] = dp_ref[i]
    qs = 4
    for q in range(0, hidden, qs):
        res = nn(rt_ref[q * seqs : (q + qs) * seqs, :], wide[...]).astype(BF)
        for e in range(qs):
            for i in range(ib):
                nl[i * seqs : (i + 1) * seqs, (q + e) * out : (q + e + 1) * out] = res[
                    e * seqs : (e + 1) * seqs, i * out : (i + 1) * out
                ]
    dl_ref[...] = nn(nl[...], wt_ref[...]).astype(BF)
    width = 512
    for w in range(0, hidden * out, width):
        dw_ref[:, w : w + width] += nn(lt_ref[...], nl[:, w : w + width])

    @pl.when(step == last)
    def _():
        to_sib.wait_send()
        for k in range(half):
            @pl.when(owner(k) == me)
            def _():
                keep(k).wait()

            @pl.when(owner(k) != me)
            def _():
                to_owner(k).wait_send()
        for k in range(half):
            @pl.when(jnp.logical_not((block == c) & (2 * k + spar == r)))
            def _():
                from_row(k).wait_recv()
        total = part[0].astype(F32)
        for k in range(1, half):
            total = total + part[k].astype(F32)
        own_ref[...] = total.astype(BF)


def update_kernel(sizes, ib, r_ref, m_ref, b_ref, dw_ref, dl_ref, o_ref, dwall_ref, dlown_ref,
                  wbuf, wsum, wall, lbuf, lsum, wsend, wrecv, gsend, grecv, lsend, lrecv, lkeep, wkeep):
    nrow, ncol = sizes
    total = nrow * ncol
    r, c, me = place(sizes)
    step = pl.program_id(0)
    last = pl.num_programs(0) - 1
    out = o_ref.shape[2]

    def scatter(k):
        to = lax.rem(me + k, total)
        return remote(dw_ref.at[to], wbuf.at[me], wsend.at[k], wrecv.at[me], to // ncol, lax.rem(to, ncol))

    def scattered(k):
        fr = lax.rem(me + k, total)
        return remote(dw_ref.at[fr], wbuf.at[fr], wsend.at[k], wrecv.at[fr], fr // ncol, lax.rem(fr, ncol))

    def gather(k):
        to = lax.rem(me + k, total)
        return remote(wsum, wall.at[me], gsend.at[k], grecv.at[me], to // ncol, lax.rem(to, ncol))

    def gathered(k):
        fr = lax.rem(me + k, total)
        return remote(wsum, wall.at[fr], gsend.at[k], grecv.at[fr], fr // ncol, lax.rem(fr, ncol))

    def left_to(k):
        to = lax.rem(c + k, ncol)
        return remote(dl_ref.at[to], lbuf.at[c], lsend.at[k], lrecv.at[c], r, to)

    def left_from(k):
        fr = lax.rem(c + k, ncol)
        return remote(dl_ref.at[fr], lbuf.at[fr], lsend.at[k], lrecv.at[fr], r, fr)

    own_left = pltpu.make_async_copy(dl_ref.at[c], lbuf.at[c], lkeep)
    own_w = pltpu.make_async_copy(dw_ref.at[me], wbuf.at[me], wkeep)

    def every(act):
        def body(k, carry):
            act(k)
            return carry

        lax.fori_loop(1, total, body, 0)

    @pl.when(step == 0)
    def _():
        own_left.start()
        own_w.start()
        greet_all(me, ncol, total)
        every(lambda k: scatter(k).start())
        for k in range(1, ncol):
            left_to(k).start()

    @pl.when(step == pl.num_programs(0) // 2)
    def _():
        own_w.wait()
        every(lambda k: scattered(k).wait_recv())
        wsum[...] = jnp.sum(wbuf[...].astype(F32), axis=0).astype(BF)
        wall[me] = wsum[...]
        every(lambda k: gather(k).start())

    for i in range(0, ib, 2):
        res = nn(r_ref[...], m_ref[:, i * out : (i + 2) * out])
        for e in range(2):
            o_ref[i + e] = (res[:, e * out : (e + 1) * out] + b_ref[...]).astype(BF)

    @pl.when(step == last)
    def _():
        own_left.wait()
        for k in range(1, ncol):
            left_from(k).wait_recv()
            left_to(k).wait_send()
        got = lbuf[0].astype(F32)
        for k in range(1, ncol):
            got = got + lbuf[k].astype(F32)
        dlown_ref[...] = got.astype(BF)
        every(lambda k: scatter(k).wait_send())
        every(lambda k: gathered(k).wait_recv())
        every(lambda k: gather(k).wait_send())
        dwall_ref[...] = wall[...]


def apply_layer_norm(x, gain, bias):
    v = x.astype(F32)
    average = jnp.mean(v, axis=-1, keepdims=True)
    shifted = v - average
    variance = jnp.mean(shifted * shifted, axis=-1, keepdims=True)
    inv = lax.rsqrt(variance + 1e-05)
    standard = shifted * inv
    return standard, inv, (standard * gain + bias).astype(BF)


def local(x, gain, bias, wl, bl, wr, br, wo, bo, dp):
    seqs, own, width = x.shape
    hidden = wl.shape[1]
    out = wo.shape[1]
    nrow, ncol = lax.axis_size("row"), lax.axis_size("col")
    sizes = (nrow, ncol)
    total = nrow * ncol
    half = nrow // 2
    rows, cols, _ = dp.shape
    qs = hidden * seqs
    qh = hidden * out
    factor = 1.0 / seqs

    standard, inv, normed = apply_layer_norm(x, gain, bias)
    both = nn(normed.reshape(-1, width), jnp.concatenate([wl, wr], axis=1))
    left = (both[:, :hidden] + bl).astype(BF).reshape(seqs, own, hidden)
    right = (both[:, hidden:] + br).astype(BF).reshape(seqs, own, hidden)
    left_t = left.transpose(2, 1, 0).reshape(hidden, own * seqs)
    right_own = right.transpose(1, 2, 0).reshape(own, qs)

    w2 = wo.reshape(hidden, qh)
    ib = divisor_up_to(rows, 4)
    steps = rows // ib
    dma = pltpu.SemaphoreType.DMA
    anywhere = pl.BlockSpec(memory_space=pl.ANY)

    def params(n):
        return pltpu.CompilerParams(
            vmem_limit_bytes=56 * 1024 * 1024, collective_id=n, has_side_effects=True
        )

    cost = pl.CostEstimate(flops=2 * cols * qs * rows * out, bytes_accessed=30000000, transcendentals=0)

    def whole(*shape):
        return pl.BlockSpec(shape, lambda t: (0,) * len(shape))

    m, dr, left_all, right_slots = pl.pallas_call(
        functools.partial(mix_kernel, sizes, ib, seqs, hidden),
        grid=(steps,),
        in_specs=[
            whole(hidden, own * seqs),
            whole(own, qs),
            whole(hidden, qh),
            pl.BlockSpec((ib, cols, out), lambda t: (t, 0, 0)),
        ],
        out_specs=[
            pl.BlockSpec((qs, ib * out), lambda t: (0, t)),
            whole(half, 2, own, qs),
            whole(hidden, rows * seqs),
            whole(nrow, own, qs),
        ],
        out_shape=[
            jax.ShapeDtypeStruct((qs, rows * out), BF),
            jax.ShapeDtypeStruct((half, 2, own, qs), BF),
            jax.ShapeDtypeStruct((hidden, rows * seqs), BF),
            jax.ShapeDtypeStruct((nrow, own, qs), BF),
        ],
        scratch_shapes=[
            pltpu.VMEM((cols, qs), F32),
            pltpu.VMEM((cols, ib * out), BF),
            pltpu.VMEM((ncol, hidden, own * seqs), BF),
            pltpu.VMEM((rows * seqs, hidden), BF),
            pltpu.VMEM((nrow, own, qs), BF),
            dma((ncol,)),
            dma((ncol,)),
            dma((half,)),
            dma((nrow,)),
            dma((half,)),
            dma,
        ],
        compiler_params=params(1),
        cost_estimate=cost,
        name="mix",
    )(left_t, right_own, w2 * BF(factor), dp)

    right_cols = right_slots.reshape(cols, qs)
    right_t = (right_cols * BF(factor)).T

    dl, dw, dr_own = pl.pallas_call(
        functools.partial(grad_kernel, sizes, ib, seqs, hidden),
        grid=(steps,),
        in_specs=[
            whole(qs, cols),
            pl.BlockSpec((ib, cols, out), lambda t: (t, 0, 0)),
            whole(qh, hidden),
            pl.BlockSpec((hidden, ib * seqs), lambda t: (0, t)),
            anywhere,
        ],
        out_specs=[
            pl.BlockSpec((ib * seqs, hidden), lambda t: (t, 0)),
            whole(hidden, qh),
            whole(own, qs),
        ],
        out_shape=[
            jax.ShapeDtypeStruct((rows * seqs, hidden), BF),
            jax.ShapeDtypeStruct((hidden, qh), F32),
            jax.ShapeDtypeStruct((own, qs), BF),
        ],
        scratch_shapes=[
            pltpu.VMEM((ib * seqs, qh), BF),
            pltpu.VMEM((cols, ib * out), BF),
            pltpu.VMEM((half, own, qs), BF),
            pltpu.VMEM((half, own, qs), BF),
            pltpu.VMEM((half, own, qs), BF),
            dma,
            dma,
            dma,
            dma((half,)),
            dma((half,)),
            dma,
        ],
        compiler_params=params(2),
        cost_estimate=cost,
        name="grad",
    )(right_t, dp, w2.T, left_all, dr)

    share = hidden * hidden // total
    dw3 = dw.astype(BF).reshape(total, share, out)
    dl3 = dl.reshape(ncol, own, seqs * hidden)
    update, dw_all, dl_own = pl.pallas_call(
        functools.partial(update_kernel, sizes, ib),
        grid=(steps,),
        in_specs=[
            whole(cols, qs),
            pl.BlockSpec((qs, ib * out), lambda t: (0, t)),
            whole(1, out),
            anywhere,
            anywhere,
        ],
        out_specs=[
            pl.BlockSpec((ib, cols, out), lambda t: (t, 0, 0)),
            whole(total, share, out),
            whole(own, seqs * hidden),
        ],
        out_shape=[
            jax.ShapeDtypeStruct((rows, cols, out), BF),
            jax.ShapeDtypeStruct((total, share, out), BF),
            jax.ShapeDtypeStruct((own, seqs * hidden), BF),
        ],
        scratch_shapes=[
            pltpu.VMEM((total, share, out), BF),
            pltpu.VMEM((share, out), BF),
            pltpu.VMEM((total, share, out), BF),
            pltpu.VMEM((ncol, own, seqs * hidden), BF),
            pltpu.VMEM((8, 128), F32),
            dma((total,)),
            dma((total,)),
            dma((total,)),
            dma((total,)),
            dma((ncol,)),
            dma((ncol,)),
            dma,
            dma,
        ],
        compiler_params=params(3),
        cost_estimate=cost,
        name="update",
    )(right_cols, m, bo.reshape(1, out), dw3, dl3)

    dl4 = dl_own.reshape(own, seqs, hidden).transpose(1, 0, 2).reshape(-1, hidden)
    dr4 = dr_own.reshape(own, hidden, seqs).transpose(2, 0, 1).reshape(-1, hidden)
    g = nt(jnp.concatenate([dl4, dr4], axis=1), jnp.concatenate([wl, wr], axis=1))
    g = g.reshape(seqs, own, width) * gain
    centre = jnp.mean(g, axis=-1, keepdims=True)
    slope = jnp.mean(g * standard, axis=-1, keepdims=True)
    dx = (inv * (g - centre - standard * slope)).astype(BF)
    return update, dx, dw_all.astype(F32).reshape(hidden * hidden, out)


def solution(mesh):
    both = ("row", "col")
    in_specs = (P(None, both, None),) + (P(),) * 8 + (P("row", "col", None),)
    out_specs = (P("row", "col", None), P(None, both, None), P())
    return jax.shard_map(local, mesh=mesh, in_specs=in_specs, out_specs=out_specs, check_vma=False)
```

```python
import functools

import jax
import jax.numpy as jnp
from jax import lax
from jax.experimental import pallas as pl
from jax.experimental.pallas import tpu as pltpu
from jax.sharding import PartitionSpec as P

BF = jnp.bfloat16
F32 = jnp.float32
MESH = pl.DeviceIdType.MESH


def divisor_up_to(total, most):
    best = 1
    for d in range(1, most + 1):
        if total % d == 0:
            best = d
    return best


def nn(a, b):
    return lax.dot_general(a, b, (((1,), (0,)), ((), ())), preferred_element_type=F32)


def nt(a, b):
    return lax.dot_general(a, b, (((1,), (1,)), ((), ())), preferred_element_type=F32)


def greet_all(me, ncol, total):
    barrier = pltpu.get_barrier_semaphore()

    def hello(k, carry):
        other = lax.rem(me + k, total)
        pl.semaphore_signal(barrier, inc=1, device_id=(other // ncol, lax.rem(other, ncol)), device_id_type=MESH)
        return carry

    lax.fori_loop(1, total, hello, 0)
    pl.semaphore_wait(barrier, total - 1)


def place(sizes):
    nrow, ncol = sizes
    r, c = lax.axis_index("row"), lax.axis_index("col")
    return r, c, r * ncol + c


def remote(src, dst, send, recv, row, col):
    return pltpu.make_async_remote_copy(
        src_ref=src, dst_ref=dst, send_sem=send, recv_sem=recv, device_id=(row, col), device_id_type=MESH
    )


def pair_kernel(sizes, ib, seqs, hidden, lt_ref, r_ref, w_ref, wt_ref, b_ref, dp_ref, o_ref, dwall_ref, dlown_ref,
                drown_ref, m_all, acc, wide, nl, lbuf, ltall, lall, rbuf, rcols, rt, drbuf, theirs, part, dwacc, dw3,
                wbuf, wsum, wall, dlbuf, dlgot, lsend, lrecv, rsend, rrecv, fsend, a_send, a_recv, b_send, b_recv,
                wsend, wrecv, gsend, grecv, dsend, drecv, local_sem):
    nrow, ncol = sizes
    half = nrow // 2
    total = nrow * ncol
    r, c, me = place(sizes)
    steps = pl.num_programs(0) // 3
    t = pl.program_id(0)
    u = lax.rem(t, steps)
    out = dp_ref.shape[2]
    own, span = r_ref.shape[0], lt_ref.shape[1]
    qs, qh = hidden * seqs, hidden * out
    par = lax.rem(r, 2)
    sib = r + 1 - 2 * par
    slot, block = lax.rem(me, nrow), me // nrow
    spar = lax.rem(slot, 2)
    place_of = r // 2
    factor = 1.0 / seqs

    def left_to(k):
        to = lax.rem(c + k, ncol)
        return remote(lt_ref, lbuf.at[c], lsend.at[k], lrecv.at[c], r, to)

    def left_from(k):
        fr = lax.rem(c + k, ncol)
        return remote(lt_ref, lbuf.at[fr], lsend.at[k], lrecv.at[fr], r, fr)

    def right_to(k):
        return remote(r_ref, rbuf.at[slot], rsend.at[k], rrecv.at[slot], 2 * k + spar, block)

    def is_me(k):
        return (block == c) & (2 * k + spar == r)

    def right_from(s):
        return remote(r_ref, rbuf.at[s], rsend.at[0], rrecv.at[s], sib, c)

    def forward(k):
        s = 2 * k + par
        return remote(rbuf.at[s], rbuf.at[s], fsend.at[k], rrecv.at[s], sib, c)

    keep = pltpu.make_async_copy(r_ref, rbuf.at[slot], local_sem.at[0])
    to_sib = remote(drbuf.at[:, 1 - par], theirs, a_send, a_recv, sib, c)

    def owner(k):
        return c * nrow + 2 * k + par

    def to_owner(k):
        g = owner(k)
        return remote(theirs.at[k], part.at[place_of], b_send.at[k], b_recv.at[place_of], g // ncol, lax.rem(g, ncol))

    def keep_part(k):
        return pltpu.make_async_copy(theirs.at[k], part.at[place_of], local_sem.at[1])

    def from_row(k):
        return remote(theirs.at[0], part.at[k], b_send.at[0], b_recv.at[k], 2 * k + spar, block)

    def scatter(k):
        to = lax.rem(me + k, total)
        return remote(dw3.at[to], wbuf.at[me], wsend.at[k], wrecv.at[me], to // ncol, lax.rem(to, ncol))

    def scattered(k):
        fr = lax.rem(me + k, total)
        return remote(dw3.at[fr], wbuf.at[fr], wsend.at[k], wrecv.at[fr], fr // ncol, lax.rem(fr, ncol))

    def gather(k):
        to = lax.rem(me + k, total)
        return remote(wsum, wall.at[me], gsend.at[k], grecv.at[me], to // ncol, lax.rem(to, ncol))

    def gathered(k):
        fr = lax.rem(me + k, total)
        return remote(wsum, wall.at[fr], gsend.at[k], grecv.at[fr], fr // ncol, lax.rem(fr, ncol))

    def dl_piece(k):
        return dlbuf.at[pl.ds(pl.multiple_of(k * span, span), span), :]

    def dl_to(k):
        to = lax.rem(c + k, ncol)
        return remote(dl_piece(to), dlgot.at[c], dsend.at[k], drecv.at[c], r, to)

    def dl_from(k):
        fr = lax.rem(c + k, ncol)
        return remote(dl_piece(fr), dlgot.at[fr], dsend.at[k], drecv.at[fr], r, fr)

    def every(act):
        def body(k, carry):
            act(k)
            return carry

        lax.fori_loop(1, total, body, 0)

    @pl.when(t == 0)
    def _():
        greet_all(me, ncol, total)
        for k in range(1, ncol):
            left_to(k).start()
        for k in range(half):
            @pl.when(is_me(k))
            def _():
                keep.start()

            @pl.when(jnp.logical_not(is_me(k)))
            def _():
                right_to(k).start()
        acc[...] = jnp.zeros_like(acc)
        dwacc[...] = jnp.zeros_like(dwacc)
        lbuf[c] = lt_ref[...]
        for k in range(1, ncol):
            left_from(k).wait_recv()
        for k in range(ncol):
            ltall[:, k * span : (k + 1) * span] = lbuf[k]
            lall[k * span : (k + 1) * span, :] = lbuf[k].astype(F32).T.astype(BF)

    def spread():
        for i in range(ib):
            wide[:, i * out : (i + 1) * out] = dp_ref[i]

    @pl.when(t < steps)
    def _():
        m_ref = m_all.at[u]
        rows = lall[pl.ds(pl.multiple_of(u * (ib * seqs), ib * seqs), ib * seqs), :]
        for q in range(0, hidden, 2):
            res = nn(rows, w_ref[:, q * out : (q + 2) * out]).astype(BF)
            for e in range(2):
                for i in range(ib):
                    m_ref[(q + e) * seqs : (q + e + 1) * seqs, i * out : (i + 1) * out] = res[
                        i * seqs : (i + 1) * seqs, e * out : (e + 1) * out
                    ]
        spread()
        width = 256
        for w in range(0, qs, width):
            acc[:, w : w + width] += nt(wide[...], m_ref[w : w + width, :])

    @pl.when(t == steps - 1)
    def _():
        for k in range(half):
            mine = c * nrow + 2 * k + par == me

            @pl.when(mine)
            def _():
                keep.wait()

            @pl.when(jnp.logical_not(mine))
            def _():
                right_from(2 * k + par).wait_recv()

            forward(k).start()
        for k in range(nrow):
            drbuf[k // 2, k % 2] = acc[k * own : (k + 1) * own, :].astype(BF)
        to_sib.start()

    @pl.when(t == steps)
    def _():
        for k in range(half):
            right_from(2 * k + 1 - par).wait_recv()
        for k in range(nrow):
            acc[k * own : (k + 1) * own, :] = rbuf[k].astype(F32)
        width = 256
        for w in range(0, qs, width):
            piece = acc[:, w : w + width]
            rcols[:, w : w + width] = piece.astype(BF)
            rt[w : w + width, :] = (piece * factor).T.astype(BF)
        to_sib.wait_recv()
        for k in range(half):
            theirs[k] = (drbuf[k, par].astype(F32) + theirs[k].astype(F32)).astype(BF)
        for k in range(half):
            @pl.when(owner(k) == me)
            def _():
                keep_part(k).start()

            @pl.when(owner(k) != me)
            def _():
                to_owner(k).start()

    @pl.when((t >= steps) & (t < 2 * steps))
    def _():
        spread()
        group = 4
        for q in range(0, hidden, group):
            res = nn(rt[q * seqs : (q + group) * seqs, :], wide[...]).astype(BF)
            for e in range(group):
                for i in range(ib):
                    nl[i * seqs : (i + 1) * seqs, (q + e) * out : (q + e + 1) * out] = res[
                        e * seqs : (e + 1) * seqs, i * out : (i + 1) * out
                    ]
        here = pl.ds(pl.multiple_of(u * (ib * seqs), ib * seqs), ib * seqs)
        dlbuf[here, :] = nn(nl[...], wt_ref[...]).astype(BF)
        width = 512
        lt_here = ltall[:, here]
        for w in range(0, qh, width):
            dwacc[:, w : w + width] += nn(lt_here, nl[:, w : w + width])

    @pl.when(t == 2 * steps - 1)
    def _():
        share = dw3.shape[1]
        per = hidden // share
        for q in range(hidden):
            for e in range(per):
                dw3[q * per + e] = dwacc[e * share : (e + 1) * share, q * out : (q + 1) * out].astype(BF)
        every(lambda k: scatter(k).start())
        for k in range(1, ncol):
            dl_to(k).start()
        wbuf[me] = dw3[me]
        dlgot[c] = dl_piece(c)[...]

    @pl.when(t == 2 * steps + (steps * 5) // 12)
    def _():
        every(lambda k: scattered(k).wait_recv())
        wsum[...] = jnp.sum(wbuf[...].astype(F32), axis=0).astype(BF)
        wall[me] = wsum[...]
        every(lambda k: gather(k).start())

    @pl.when(t >= 2 * steps)
    def _():
        m_ref = m_all.at[u]
        for i in range(0, ib, 2):
            res = nn(rcols[...], m_ref[:, i * out : (i + 2) * out])
            for e in range(2):
                o_ref[i + e] = (res[:, e * out : (e + 1) * out] + b_ref[...]).astype(BF)

    @pl.when(t == 3 * steps - 1)
    def _():
        for k in range(1, ncol):
            left_to(k).wait_send()
            dl_from(k).wait_recv()
            dl_to(k).wait_send()
        got = dlgot[0].astype(F32)
        for k in range(1, ncol):
            got = got + dlgot[k].astype(F32)
        dlown_ref[...] = got.astype(BF)
        to_sib.wait_send()
        for k in range(half):
            forward(k).wait_send()

            @pl.when(jnp.logical_not(is_me(k)))
            def _():
                right_to(k).wait_send()

            @pl.when(owner(k) == me)
            def _():
                keep_part(k).wait()

            @pl.when(owner(k) != me)
            def _():
                to_owner(k).wait_send()
        for k in range(half):
            @pl.when(jnp.logical_not(is_me(k)))
            def _():
                from_row(k).wait_recv()
        summed = part[0].astype(F32)
        for k in range(1, half):
            summed = summed + part[k].astype(F32)
        drown_ref[...] = summed.astype(BF)
        every(lambda k: scatter(k).wait_send())
        every(lambda k: gathered(k).wait_recv())
        every(lambda k: gather(k).wait_send())
        dwall_ref[...] = wall[...]


def apply_layer_norm(x, gain, bias):
    v = x.astype(F32)
    average = jnp.mean(v, axis=-1, keepdims=True)
    shifted = v - average
    variance = jnp.mean(shifted * shifted, axis=-1, keepdims=True)
    inv = lax.rsqrt(variance + 1e-05)
    standard = shifted * inv
    return standard, inv, (standard * gain + bias).astype(BF)


def local(x, gain, bias, wl, bl, wr, br, wo, bo, dp):
    seqs, own, width = x.shape
    hidden = wl.shape[1]
    out = wo.shape[1]
    nrow, ncol = lax.axis_size("row"), lax.axis_size("col")
    sizes = (nrow, ncol)
    total = nrow * ncol
    half = nrow // 2
    rows, cols, _ = dp.shape
    qs = hidden * seqs
    qh = hidden * out
    factor = 1.0 / seqs

    standard, inv, normed = apply_layer_norm(x, gain, bias)
    both = nn(normed.reshape(-1, width), jnp.concatenate([wl, wr], axis=1))
    left = (both[:, :hidden] + bl).astype(BF).reshape(seqs, own, hidden)
    right = (both[:, hidden:] + br).astype(BF).reshape(seqs, own, hidden)
    left_t = left.transpose(2, 1, 0).reshape(hidden, own * seqs)
    right_own = right.transpose(1, 2, 0).reshape(own, qs)

    w2 = wo.reshape(hidden, qh)
    ib = divisor_up_to(rows, 4)
    steps = rows // ib
    dma = pltpu.SemaphoreType.DMA

    def params(n):
        return pltpu.CompilerParams(
            vmem_limit_bytes=56 * 1024 * 1024, collective_id=n, has_side_effects=True
        )

    cost = pl.CostEstimate(flops=8 * cols * qs * rows * out, bytes_accessed=30000000, transcendentals=0)

    def whole(*shape):
        return pl.BlockSpec(shape, lambda t: (0,) * len(shape))

    share = hidden * hidden // total
    update, dw_all, dl_own, dr_own = pl.pallas_call(
        functools.partial(pair_kernel, sizes, ib, seqs, hidden),
        grid=(3 * steps,),
        in_specs=[
            whole(hidden, own * seqs),
            whole(own, qs),
            whole(hidden, qh),
            whole(qh, hidden),
            whole(1, out),
            pl.BlockSpec(
                (ib, cols, out), lambda t: (jnp.where(t < 2 * steps, lax.rem(t, steps), steps - 1), 0, 0)
            ),
        ],
        out_specs=[
            pl.BlockSpec((ib, cols, out), lambda t: (jnp.maximum(t - 2 * steps, 0), 0, 0)),
            whole(total, share, out),
            whole(own * seqs, hidden),
            whole(own, qs),
        ],
        out_shape=[
            jax.ShapeDtypeStruct((rows, cols, out), BF),
            jax.ShapeDtypeStruct((total, share, out), BF),
            jax.ShapeDtypeStruct((own * seqs, hidden), BF),
            jax.ShapeDtypeStruct((own, qs), BF),
        ],
        scratch_shapes=[
            pltpu.VMEM((steps, qs, ib * out), BF),
            pltpu.VMEM((cols, qs), F32),
            pltpu.VMEM((cols, ib * out), BF),
            pltpu.VMEM((ib * seqs, qh), BF),
            pltpu.VMEM((ncol, hidden, own * seqs), BF),
            pltpu.VMEM((hidden, rows * seqs), BF),
            pltpu.VMEM((rows * seqs, hidden), BF),
            pltpu.VMEM((nrow, own, qs), BF),
            pltpu.VMEM((cols, qs), BF),
            pltpu.VMEM((qs, cols), BF),
            pltpu.VMEM((half, 2, own, qs), BF),
            pltpu.VMEM((half, own, qs), BF),
            pltpu.VMEM((half, own, qs), BF),
            pltpu.VMEM((hidden, qh), F32),
            pltpu.VMEM((total, share, out), BF),
            pltpu.VMEM((total, share, out), BF),
            pltpu.VMEM((share, out), BF),
            pltpu.VMEM((total, share, out), BF),
            pltpu.VMEM((rows * seqs, hidden), BF),
            pltpu.VMEM((ncol, own * seqs, hidden), BF),
            dma((ncol,)),
            dma((ncol,)),
            dma((half,)),
            dma((nrow,)),
            dma((half,)),
            dma,
            dma,
            dma((half,)),
            dma((half,)),
            dma((total,)),
            dma((total,)),
            dma((total,)),
            dma((total,)),
            dma((ncol,)),
            dma((ncol,)),
            dma((2,)),
        ],
        compiler_params=params(1),
        cost_estimate=cost,
        name="pair",
    )(left_t, right_own, w2 * BF(factor), w2.T, bo.reshape(1, out), dp)

    dl4 = dl_own.reshape(own, seqs, hidden).transpose(1, 0, 2).reshape(-1, hidden)
    dr4 = dr_own.reshape(own, hidden, seqs).transpose(2, 0, 1).reshape(-1, hidden)
    g = nt(jnp.concatenate([dl4, dr4], axis=1), jnp.concatenate([wl, wr], axis=1))
    g = g.reshape(seqs, own, width) * gain
    centre = jnp.mean(g, axis=-1, keepdims=True)
    slope = jnp.mean(g * standard, axis=-1, keepdims=True)
    dx = (inv * (g - centre - standard * slope)).astype(BF)
    dw_out = dw_all.reshape(hidden, hidden, out).transpose(1, 0, 2).astype(F32)
    return update, dx, dw_out.reshape(hidden * hidden, out)


def solution(mesh):
    both = ("row", "col")
    in_specs = (P(None, both, None),) + (P(),) * 8 + (P("row", "col", None),)
    out_specs = (P("row", "col", None), P(None, both, None), P())
    return jax.shard_map(local, mesh=mesh, in_specs=in_specs, out_specs=out_specs, check_vma=False)
```
